32 devices in a mesh: ctx: 4 (over y, x), req: 8 (over z, core).
Axes of the slice: x: 2, y: 2, z: 4, core: 2. Of those that a mesh axis runs over, the one named last changes fastest.
Arguments:
- queries: bfloat16 [512, 64, 128], P('req', 'ctx'), may hold values from -96 to 96
- prefix_keys: bfloat16 [8192, 1024], P('ctx'), may hold values from -9 to 9
- lengths: int32 [32], P('req'), may hold values from 1024 to 8192, as said below
- positions: int32 [32, 16], P('req'), may hold values from 2 to 10240, as said below
- pool_width: int32 [8], replicated, may hold values from 1 to 7, as said below
- scorer_in: bfloat16 [1024, 1024], replicated, may hold values from -0.1875 to 0.1875
- scorer_out: bfloat16 [1024, 8], replicated, may hold values from -0.1875 to 0.1875
Outputs:
- importance: float32 [8, 8192], P(None, ('ctx', 'req'))
The draws below stay inside these ranges and needn't reach their ends.
Inputs may be any that keep to these rules, and one draw needn't show every extreme that they name: `lengths`: some request's length is exactly 8192 and some other's exactly 1024. `positions`: each is 2 or more and lies within 2048 of its request's length. `pool_width`: some key head's width is exactly 7 and some other's exactly 1.
All inputs are finite; a program needn't handle non-finite values.
Results may differ from the reference program's by a relative error of at most 0.0003.
The reference program's roundings to bfloat16 on the way (of `hidden`) count: a program that leaves them out, or rounds other values in their place, can miss the bound.
Values may be sent and summed in bfloat16 or wider, within the bound.
A program may use at most 64 MiB of HBM per device.

```python
import math
import jax
import jax.numpy as jnp
from jax import lax

HEADS = 64
KVH = 8
HDIM = 128
GROUP = 8
WIN = 16
SHID = 1024
RAD = 3
KEY_DEV = 2048
REQS = 32
KEYS = 8192


def base_keys(key):
    noise_key = jax.random.fold_in(jax.random.fold_in(key, 101), 0)
    values = jax.random.truncated_normal(noise_key, -6.0, 6.0, (KEYS, KVH * HDIM), jnp.float32)
    return values


def draw_prefix_keys(key, part):
    return base_keys(key).astype(jnp.bfloat16)


def draw_queries(key, part):
    noise_key = jax.random.fold_in(jax.random.fold_in(key, 202), 0)
    values = jax.random.truncated_normal(noise_key, -6.0, 6.0, (REQS * WIN, HEADS, HDIM), jnp.float32)
    return values.astype(jnp.bfloat16)


def request_spans(key):
    long_key, modest_key, chance_key, choose_key, jitter_key = jax.random.split(jax.random.fold_in(key, 303), 5)
    modest = jax.random.randint(modest_key, (REQS,), KEYS // 8, KEYS // 2 + 1)
    longer = jax.random.randint(long_key, (REQS,), KEYS // 2, KEYS + 1)
    chance = jax.random.randint(chance_key, (REQS,), 0, 8) == 0
    lengths = jnp.where(chance, longer, modest)
    chosen = jax.random.randint(choose_key, (), 0, REQS)
    shortest = (chosen + 1) % REQS
    request_index = jnp.arange(REQS)
    lengths = jnp.where(request_index == chosen, KEYS, lengths)
    lengths = jnp.where(request_index == shortest, KEYS // 8, lengths)
    jitter = jax.random.randint(jitter_key, (REQS, WIN), -KEY_DEV, KEY_DEV + 1)
    positions = jnp.maximum(lengths[:, None] + jitter, 2)
    window_index = jnp.arange(WIN)
    top_slot = (request_index[:, None] == chosen) & (window_index[None, :] == WIN - 1)
    low_slot = (request_index[:, None] == shortest) & (window_index[None, :] == 0)
    positions = jnp.where(top_slot, KEYS + KEY_DEV, positions)
    positions = jnp.where(low_slot, max(2, KEYS // 8 - KEY_DEV), positions)
    return (lengths.astype(jnp.int32), positions.astype(jnp.int32))


def draw_lengths(key, part):
    return request_spans(key)[0]


def draw_positions(key, part):
    return request_spans(key)[1]


def draw_pool_width(key, part):
    width_key, head_key = jax.random.split(jax.random.fold_in(key, 404))
    widths = jax.random.randint(width_key, (KVH,), 1, 2 * RAD + 2)
    widest = jax.random.randint(head_key, (), 0, KVH)
    narrowest = (widest + 1) % KVH
    head_index = jnp.arange(KVH)
    widths = jnp.where(head_index == widest, 2 * RAD + 1, widths)
    widths = jnp.where(head_index == narrowest, 1, widths)
    return widths.astype(jnp.int32)


def scatter_about(own_key, shape, spread, bound, dtype=jnp.bfloat16):
    return jnp.clip(spread * jax.random.normal(own_key, shape, jnp.float32), -bound, bound).astype(dtype)


def setup_inputs(seed: int = 0) -> dict:
    seeds = jax.random.split(jax.random.key(seed), 8)
    queries = draw_queries(jax.random.fold_in(seeds[7], 71), 0)
    prefix_keys = draw_prefix_keys(jax.random.fold_in(seeds[7], 71), 0)
    lengths = draw_lengths(jax.random.fold_in(seeds[7], 71), 0)
    positions = draw_positions(jax.random.fold_in(seeds[7], 71), 0)
    pool_width = draw_pool_width(jax.random.fold_in(seeds[7], 71), 0)
    scorer_in = scatter_about(seeds[5], (KVH * HDIM, SHID), (KVH * HDIM) ** -0.5, 0.1875)
    scorer_out = scatter_about(seeds[6], (SHID, KVH), SHID ** -0.5, 0.1875)
    return dict(queries=queries, prefix_keys=prefix_keys, lengths=lengths, positions=positions, pool_width=pool_width, scorer_in=scorer_in, scorer_out=scorer_out)


MASKED = -1e+30

def reference(queries, prefix_keys, lengths, positions, pool_width, scorer_in, scorer_out):
    keyed = prefix_keys.reshape(KEYS, KVH, HDIM).astype(jnp.float32)
    key_index = lax.iota(jnp.int32, KEYS)
    limits = jnp.minimum(positions, lengths[:, None] - 1).astype(jnp.int32)
    grouped = queries.reshape(REQS, WIN, KVH, GROUP, HDIM)

    def per_request(totals, inputs):
        query_block, limit_row = inputs
        scores = jnp.einsum('wvgd,kvd->vwgk', query_block.astype(jnp.float32), keyed) * (1.0 / math.sqrt(HDIM))
        visible = key_index[None, :] <= limit_row[:, None]
        scores = jnp.where(visible[None, :, None, :], scores, MASKED)
        highest = lax.optimization_barrier(jnp.max(scores, axis=-1, keepdims=True))
        weights = jnp.exp(scores - highest)
        total = lax.optimization_barrier(jnp.sum(weights, axis=-1, keepdims=True))
        return (totals + lax.optimization_barrier(jnp.sum(weights / total, axis=(1, 2))), None)
    columns = lax.scan(per_request, jnp.zeros((KVH, KEYS), jnp.float32), (grouped, limits))[0]
    padded = jnp.pad(columns, ((0, 0), (RAD, RAD)))
    window_sum = jnp.zeros_like(columns)
    for tap_offset in range(-RAD, RAD + 1):
        inside = (tap_offset >= -(pool_width // 2)) & (tap_offset <= (pool_width - 1) // 2)
        window_sum = window_sum + jnp.where(inside[:, None], padded[:, RAD + tap_offset:RAD + tap_offset + KEYS], 0.0)
    pooled = window_sum / pool_width.astype(jnp.float32)[:, None]
    projected = jnp.dot(prefix_keys.astype(jnp.float32), scorer_in.astype(jnp.float32), precision=lax.Precision.HIGHEST)
    hidden = jax.nn.silu(projected).astype(jnp.bfloat16)
    gating = jnp.dot(hidden.astype(jnp.float32), scorer_out.astype(jnp.float32), precision=lax.Precision.HIGHEST)
    return pooled * (2.0 * jax.nn.sigmoid(gating.T))
```

```python
import functools
import math

import jax
import jax.numpy as jnp
from jax import lax
from jax.experimental import pallas as pl
from jax.experimental.pallas import tpu as pltpu
from jax.sharding import PartitionSpec as P

RAD = 3
MASKED = -1e30
LANES = 128
SUB = 8
MESH = pl.DeviceIdType.MESH


def kernel(
    sizes, q_ref, limits_ref, width_ref, scorer_out_ref, keys_hbm, scorer_in_hbm, out_ref,
    keys, scorer_in, q_all, bias, onehot, scores, exps, stats, columns, pieces, parts, left, right,
    ext, gate,
    keys_sem, scorer_sem, own_sem, q_send, q_recv, stat_send, stat_recv, part_send, part_recv,
    left_send, left_recv, right_send, right_recv,
):
    ctx, req, units, split, side = sizes
    ctx_me, req_me = lax.axis_index("ctx"), lax.axis_index("req")
    key_heads = width_ref.shape[0]
    key_dev = keys.shape[0]
    head_dim = q_ref.shape[2]
    unit_rows = q_ref.shape[1]
    groups = unit_rows // SUB
    owned = out_ref.shape[1]
    factor = math.log2(math.e) / math.sqrt(head_dim)

    def source(step):
        down, along = step // side, step % side
        row = (ctx_me // side + down) % (ctx // side)
        return row * side + (ctx_me % side + along) % side

    def ring(step):
        return (req_me + step) % req

    keys_copy = pltpu.make_async_copy(keys_hbm, keys, keys_sem)
    keys_copy.start()
    scorer_copy = pltpu.make_async_copy(scorer_in_hbm, scorer_in, scorer_sem)
    scorer_copy.start()
    own_copy = pltpu.make_async_copy(q_ref, q_all.at[ctx_me], own_sem)
    own_copy.start()

    barrier = pltpu.get_barrier_semaphore()

    def greet(c, r):
        pl.semaphore_signal(barrier, inc=1, device_id=(c, r), device_id_type=MESH)

    for step in range(1, ctx):
        greet(source(step), req_me)
    for step in range(1, req):
        greet(ctx_me, ring(step))

    has_left = ctx_me > 0
    has_right = ctx_me < ctx - 1
    takes_left = jnp.logical_and(req_me == 0, has_left)
    takes_right = jnp.logical_and(req_me == req - 1, has_right)

    @pl.when(takes_left)
    def _():
        for r in range(1, req):
            greet(ctx_me - 1, r)

    @pl.when(takes_right)
    def _():
        for r in range(req - 1):
            greet(ctx_me + 1, r)

    extra_right = jnp.logical_and(has_right, req_me != 0)
    extra_left = jnp.logical_and(has_left, req_me != req - 1)
    extra = extra_right.astype(jnp.int32) + extra_left.astype(jnp.int32)
    pl.semaphore_wait(barrier, ctx - 1 + req - 1 + extra)

    def q_copy(unit, step):
        return pltpu.make_async_remote_copy(
            src_ref=q_ref.at[unit], dst_ref=q_all.at[ctx_me, unit],
            send_sem=q_send.at[unit, step], recv_sem=q_recv.at[ctx_me, unit],
            device_id=(source(step), req_me), device_id_type=MESH,
        )

    def q_arrival(unit, who):
        return pltpu.make_async_remote_copy(
            src_ref=q_ref.at[unit], dst_ref=q_all.at[who, unit],
            send_sem=q_send.at[unit, 0], recv_sem=q_recv.at[who, unit],
            device_id=(who, req_me), device_id_type=MESH,
        )

    for unit in range(units):
        for step in range(1, ctx):
            q_copy(unit, step).start()

    lane_keys = ctx_me * key_dev + lax.broadcasted_iota(jnp.int32, (key_dev, LANES), 0)
    bias[...] = jnp.where(lane_keys <= limits_ref[...], 0.0, MASKED).astype(jnp.bfloat16)
    row = lax.broadcasted_iota(jnp.int32, (unit_rows, LANES), 0)
    lane = lax.broadcasted_iota(jnp.int32, (unit_rows, LANES), 1)
    first = lane * split
    onehot[...] = jnp.where(
        jnp.logical_and(row >= first, row < first + split), 1.0, 0.0
    ).astype(jnp.bfloat16)
    columns[...] = jnp.zeros_like(columns)
    own_copy.wait()
    keys_copy.wait()

    tile_lane = lax.broadcasted_iota(jnp.int32, (SUB, LANES), 1)

    def key_head(who, unit):
        return ((who * units + unit) * split) // (units_heads)

    units_heads = (ctx * units * split) // key_heads

    def stat_copy(step, peer):
        who = source(step)
        return pltpu.make_async_remote_copy(
            src_ref=stats.at[ctx_me, who], dst_ref=stats.at[ctx_me, who],
            send_sem=stat_send.at[step, peer], recv_sem=stat_recv.at[ctx_me, who],
            device_id=(source(peer), req_me), device_id_type=MESH,
        )

    def stat_arrival(peer, who):
        other = source(peer)
        return pltpu.make_async_remote_copy(
            src_ref=stats.at[other, who], dst_ref=stats.at[other, who],
            send_sem=stat_send.at[0, 0], recv_sem=stat_recv.at[other, who],
            device_id=(other, req_me), device_id_type=MESH,
        )

    def score_step(step, carry):
        who = source(step)

        def score_unit(unit, carry):
            @pl.when(step > 0)
            def _():
                q_arrival(unit, who).wait_recv()

            head = key_head(who, unit)
            rows = jnp.concatenate([q_all[who, unit], onehot[...]], axis=1)
            width = min(512, key_dev)
            for start in range(0, key_dev, width):
                block = jnp.concatenate(
                    [
                        keys[start : start + width, pl.ds(pl.multiple_of(head * head_dim, LANES), head_dim)],
                        bias[start : start + width, :],
                    ],
                    axis=1,
                )
                scores[:, start : start + width] = lax.dot_general(
                    rows, block, (((1,), (1,)), ((), ())), preferred_element_type=jnp.float32
                )
            slot = step * units + unit

            def chunk(index, running):
                top, total = running
                for k in range(8):
                    group = index * 8 + k
                    span = pl.ds(pl.multiple_of(group * SUB, SUB), SUB)
                    s = scores[span, :]
                    highest = jnp.max(s, axis=1, keepdims=True)
                    e = jnp.exp2((s - highest) * factor)
                    exps[slot, span, :] = e
                    here = tile_lane == group
                    top = jnp.where(here, highest, top)
                    total = jnp.where(here, jnp.sum(e, axis=1, keepdims=True), total)
                return top, total

            top, total = lax.fori_loop(
                0, groups // 8, chunk,
                (jnp.zeros((SUB, LANES), jnp.float32), jnp.ones((SUB, LANES), jnp.float32)),
            )
            stats[ctx_me, who, unit, 0] = top
            stats[ctx_me, who, unit, 1] = total
            return carry

        lax.fori_loop(0, units, score_unit, 0)
        for peer in range(1, ctx):
            stat_copy(step, peer).start()
        return carry

    lax.fori_loop(0, ctx, score_step, 0)

    scorer_copy.wait()
    mine = keys[pl.ds(pl.multiple_of(req_me * owned, owned), owned), :]
    projected = jnp.dot(mine, scorer_in[...], preferred_element_type=jnp.float32)
    hidden = (projected / (1.0 + jnp.exp(-projected))).astype(jnp.bfloat16)
    gating = lax.dot_general(
        scorer_out_ref[...], hidden, (((1,), (1,)), ((), ())), preferred_element_type=jnp.float32
    )
    gate[...] = 2.0 / (1.0 + jnp.exp(-gating))

    def mass_step(step, carry):
        who = source(step)
        for peer in range(1, ctx):
            stat_arrival(peer, who).wait_recv()

        def mass_unit(unit, carry):
            highest = stats[0, who, unit, 0]
            for other in range(1, ctx):
                highest = jnp.maximum(highest, stats[other, who, unit, 0])
            total = jnp.zeros((SUB, LANES), jnp.float32)
            for other in range(ctx):
                total = total + stats[other, who, unit, 1] * jnp.exp2(
                    (stats[other, who, unit, 0] - highest) * factor
                )
            weight = jnp.exp2((stats[ctx_me, who, unit, 0] - highest) * factor) / total
            slot = step * units + unit

            def chunk(index, running):
                mass, weight = running
                for k in range(8):
                    span = pl.ds(pl.multiple_of((index * 8 + k) * SUB, SUB), SUB)
                    mass = mass + exps[slot, span, :] * weight[:, k : k + 1]
                return mass, pltpu.roll(weight, LANES - 8, 1)

            mass, _ = lax.fori_loop(
                0, groups // 8, chunk, (jnp.zeros((SUB, key_dev), jnp.float32), weight)
            )
            head = key_head(who, unit)
            columns[pl.ds(head, 1), :] += jnp.sum(mass, axis=0, keepdims=True)
            return carry

        return lax.fori_loop(0, units, mass_unit, carry)

    lax.fori_loop(0, ctx, mass_step, 0)

    shifted = pltpu.roll(
        jnp.concatenate([columns[...], jnp.zeros((key_heads, LANES), jnp.float32)], axis=1), RAD, 1
    )
    for r in range(req):
        pieces[r] = shifted[:, r * owned : (r + 1) * owned + LANES]

    def part_copy(step):
        to = ring(step)
        return pltpu.make_async_remote_copy(
            src_ref=pieces.at[to], dst_ref=parts.at[req_me],
            send_sem=part_send.at[step], recv_sem=part_recv.at[req_me],
            device_id=(ctx_me, to), device_id_type=MESH,
        )

    def part_arrival(step):
        other = ring(step)
        return pltpu.make_async_remote_copy(
            src_ref=pieces.at[other], dst_ref=parts.at[other],
            send_sem=part_send.at[0], recv_sem=part_recv.at[other],
            device_id=(ctx_me, other), device_id_type=MESH,
        )

    def left_copy():
        return pltpu.make_async_remote_copy(
            src_ref=pieces.at[req - 1, :, pl.ds(owned, LANES)], dst_ref=left.at[req_me],
            send_sem=left_send, recv_sem=left_recv.at[req_me],
            device_id=(ctx_me + 1, 0), device_id_type=MESH,
        )

    def right_copy():
        return pltpu.make_async_remote_copy(
            src_ref=pieces.at[0, :, pl.ds(0, LANES)], dst_ref=right.at[req_me],
            send_sem=right_send, recv_sem=right_recv.at[req_me],
            device_id=(ctx_me - 1, req - 1), device_id_type=MESH,
        )

    for step in range(1, req):
        part_copy(step).start()

    @pl.when(has_right)
    def _():
        left_copy().start()

    @pl.when(has_left)
    def _():
        right_copy().start()

    for step in range(1, req):
        part_arrival(step).wait_recv()
    summed = pieces[req_me]
    for step in range(1, req):
        summed = summed + parts[ring(step)]
    ext[...] = summed

    @pl.when(takes_left)
    def _():
        total = jnp.zeros((key_heads, LANES), jnp.float32)
        for r in range(req):
            pltpu.make_async_remote_copy(
                src_ref=left.at[r], dst_ref=left.at[r], send_sem=left_send,
                recv_sem=left_recv.at[r], device_id=(ctx_me - 1, r), device_id_type=MESH,
            ).wait_recv()
            total = total + left[r]
        ext[:, :LANES] += total

    @pl.when(takes_right)
    def _():
        total = jnp.zeros((key_heads, LANES), jnp.float32)
        for r in range(req):
            pltpu.make_async_remote_copy(
                src_ref=right.at[r], dst_ref=right.at[r], send_sem=right_send,
                recv_sem=right_recv.at[r], device_id=(ctx_me + 1, r), device_id_type=MESH,
            ).wait_recv()
            total = total + right[r]
        halo_lane = lax.broadcasted_iota(jnp.int32, (key_heads, LANES), 1)
        inside = jnp.logical_and(halo_lane >= RAD, halo_lane < 2 * RAD)
        ext[:, owned:] += jnp.where(inside, total, 0.0)

    pool_width = width_ref[...]
    half = pool_width // 2
    rest = (pool_width - 1) // 2
    whole = ext[...]
    window = jnp.zeros((key_heads, owned), jnp.float32)
    for tap in range(-RAD, RAD + 1):
        moved = whole if tap == -RAD else pltpu.roll(whole, owned + LANES - RAD - tap, 1)
        inside = jnp.logical_and(tap >= -half, tap <= rest)
        window = window + jnp.where(inside, moved[:, :owned], 0.0)
    out_ref[...] = window / pool_width.astype(jnp.float32) * gate[...]

    for unit in range(units):
        for step in range(1, ctx):
            q_copy(unit, step).wait_send()

    def drain(step, carry):
        for peer in range(1, ctx):
            stat_copy(step, peer).wait_send()
        return carry

    lax.fori_loop(0, ctx, drain, 0)
    for step in range(1, req):
        part_copy(step).wait_send()

    @pl.when(has_right)
    def _():
        left_copy().wait_send()

    @pl.when(has_left)
    def _():
        right_copy().wait_send()


def per_device(
    ctx, req, queries, prefix_keys, lengths, positions, pool_width, scorer_in, scorer_out
):
    row_count, heads_here, head_dim = queries.shape
    key_heads = pool_width.shape[0]
    key_dev = prefix_keys.shape[0]
    group = heads_here * ctx // key_heads
    split = min(group, heads_here)
    units = heads_here // split
    unit_rows = row_count * split
    owned = key_dev // req
    side = math.isqrt(ctx)
    side = side if side * side == ctx else 1
    arranged = (
        queries.reshape(row_count, units, split, head_dim)
        .transpose(1, 0, 2, 3)
        .reshape(units, unit_rows, head_dim)
    )
    limits = jnp.minimum(positions, lengths[:, None] - 1).reshape(1, row_count)
    limits = jnp.pad(limits, ((0, 0), (0, LANES - row_count)))
    vmem = pl.BlockSpec(memory_space=pltpu.VMEM)
    anywhere = pl.BlockSpec(memory_space=pl.ANY)
    dma = pltpu.SemaphoreType.DMA
    f32, bf16 = jnp.float32, jnp.bfloat16
    return pl.pallas_call(
        functools.partial(kernel, (ctx, req, units, split, side)),
        out_shape=jax.ShapeDtypeStruct((key_heads, owned), f32),
        in_specs=[vmem, vmem, vmem, vmem, anywhere, anywhere],
        out_specs=vmem,
        scratch_shapes=[
            pltpu.VMEM(prefix_keys.shape, bf16),
            pltpu.VMEM(scorer_in.shape, bf16),
            pltpu.VMEM((ctx, units, unit_rows, head_dim), bf16),
            pltpu.VMEM((key_dev, LANES), bf16),
            pltpu.VMEM((unit_rows, LANES), bf16),
            pltpu.VMEM((unit_rows, key_dev), f32),
            pltpu.VMEM((ctx * units, unit_rows, key_dev), f32),
            pltpu.VMEM((ctx, ctx, units, 2, SUB, LANES), f32),
            pltpu.VMEM((key_heads, key_dev), f32),
            pltpu.VMEM((req, key_heads, owned + LANES), f32),
            pltpu.VMEM((req, key_heads, owned + LANES), f32),
            pltpu.VMEM((req, key_heads, LANES), f32),
            pltpu.VMEM((req, key_heads, LANES), f32),
            pltpu.VMEM((key_heads, owned + LANES), f32),
            pltpu.VMEM((key_heads, owned), f32),
            dma, dma, dma,
            dma((units, ctx)), dma((ctx, units)),
            dma((ctx, ctx)), dma((ctx, ctx)),
            dma((req,)), dma((req,)),
            dma, dma((req,)),
            dma, dma((req,)),
        ],
        compiler_params=pltpu.CompilerParams(
            collective_id=0, has_side_effects=True, vmem_limit_bytes=60 * 1024 * 1024
        ),
    )(arranged, limits, pool_width[:, None], scorer_out.T, prefix_keys, scorer_in)


def solution(mesh):
    placed = (P("req", "ctx", None), P("ctx", None), P("req"), P("req", None), P(), P(), P())
    body = functools.partial(per_device, mesh.shape["ctx"], mesh.shape["req"])
    return jax.shard_map(
        body, mesh=mesh, in_specs=placed, out_specs=P(None, ("ctx", "req")), check_vma=False
    )
```

```python
import functools
import math

import jax
import jax.numpy as jnp
from jax import lax
from jax.experimental import pallas as pl
from jax.experimental.pallas import tpu as pltpu
from jax.sharding import PartitionSpec as P

RAD = 3
MASKED = -1e30
LANES = 128
SUB = 8
MESH = pl.DeviceIdType.MESH


def kernel(
    sizes, q_ref, lengths_ref, positions_ref, width_ref, scorer_out_ref, keys_hbm, scorer_in_hbm, out_ref,
    keys, scorer_in, q_all, limits, bias, onehot, scores_a, scores_b, exps, stats, columns, pieces, parts, left, right,
    ext, gate,
    keys_sem, scorer_sem, own_sem, q_send, q_recv, stat_send, stat_recv, part_send, part_recv,
    left_send, left_recv, right_send, right_recv,
):
    ctx, req, units, split, side = sizes
    ctx_me, req_me = lax.axis_index("ctx"), lax.axis_index("req")
    key_heads = width_ref.shape[0]
    key_dev = keys.shape[0]
    head_dim = q_ref.shape[2]
    unit_rows = q_ref.shape[1]
    groups = unit_rows // SUB
    owned = out_ref.shape[1]
    factor = math.log2(math.e) / math.sqrt(head_dim)

    def source(step):
        down, along = step // side, step % side
        row = (ctx_me // side + down) % (ctx // side)
        return row * side + (ctx_me % side + along) % side

    def ring(step):
        return (req_me + step) % req

    slots = ctx * units
    heads_each = slots * split // key_heads

    def key_head(slot):
        return ((source(slot // units) * units + slot % units) * split) // heads_each

    def keys_copy(index):
        head = key_head(index) if slots == key_heads else index
        span = pl.ds(pl.multiple_of(head * head_dim, LANES), head_dim)
        return pltpu.make_async_copy(keys_hbm.at[:, span], keys.at[:, span], keys_sem.at[index])

    for index in range(key_heads):
        keys_copy(index).start()
    scorer_copy = pltpu.make_async_copy(scorer_in_hbm, scorer_in, scorer_sem)
    scorer_copy.start()
    own_copy = pltpu.make_async_copy(q_ref, q_all.at[ctx_me], own_sem)
    own_copy.start()

    barrier = pltpu.get_barrier_semaphore()

    def greet(c, r):
        pl.semaphore_signal(barrier, inc=1, device_id=(c, r), device_id_type=MESH)

    for step in range(1, ctx):
        greet(source(step), req_me)
    for step in range(1, req):
        greet(ctx_me, ring(step))

    has_left = ctx_me > 0
    has_right = ctx_me < ctx - 1
    takes_left = jnp.logical_and(req_me == 0, has_left)
    takes_right = jnp.logical_and(req_me == req - 1, has_right)

    @pl.when(takes_left)
    def _():
        for r in range(1, req):
            greet(ctx_me - 1, r)

    @pl.when(takes_right)
    def _():
        for r in range(req - 1):
            greet(ctx_me + 1, r)

    extra_right = jnp.logical_and(has_right, req_me != 0)
    extra_left = jnp.logical_and(has_left, req_me != req - 1)
    extra = extra_right.astype(jnp.int32) + extra_left.astype(jnp.int32)
    pl.semaphore_wait(barrier, ctx - 1 + req - 1 + extra)

    def q_copy(unit, step):
        return pltpu.make_async_remote_copy(
            src_ref=q_ref.at[unit], dst_ref=q_all.at[ctx_me, unit],
            send_sem=q_send.at[unit, step], recv_sem=q_recv.at[ctx_me, unit],
            device_id=(source(step), req_me), device_id_type=MESH,
        )

    def q_arrival(unit, who):
        return pltpu.make_async_remote_copy(
            src_ref=q_ref.at[unit], dst_ref=q_all.at[who, unit],
            send_sem=q_send.at[unit, 0], recv_sem=q_recv.at[who, unit],
            device_id=(who, req_me), device_id_type=MESH,
        )

    for unit in range(units):
        for step in range(1, ctx):
            q_copy(unit, step).start()

    lane_keys = ctx_me * key_dev + lax.broadcasted_iota(jnp.int32, (key_dev, LANES), 0)
    requests, window_rows = positions_ref.shape
    limits[...] = jnp.zeros_like(limits)
    for i in range(requests):
        limits[i : i + 1, :window_rows] = jnp.minimum(
            positions_ref[i : i + 1, :], lengths_ref[i] - 1
        )
    limit = limits[0:1, :]
    for i in range(1, requests):
        limit = limit + pltpu.roll(limits[i : i + 1, :], i * window_rows, 1)
    bias[...] = jnp.where(lane_keys <= limit, 0.0, MASKED).astype(jnp.bfloat16)
    row = lax.broadcasted_iota(jnp.int32, (unit_rows, LANES), 0)
    lane = lax.broadcasted_iota(jnp.int32, (unit_rows, LANES), 1)
    first = lane * split
    onehot[...] = jnp.where(
        jnp.logical_and(row >= first, row < first + split), 1.0, 0.0
    ).astype(jnp.bfloat16)
    columns[...] = jnp.zeros_like(columns)
    own_copy.wait()

    tile_lane = lax.broadcasted_iota(jnp.int32, (SUB, LANES), 1)

    def stat_copy(step, peer):
        who = source(step)
        return pltpu.make_async_remote_copy(
            src_ref=stats.at[ctx_me, who], dst_ref=stats.at[ctx_me, who],
            send_sem=stat_send.at[step, peer], recv_sem=stat_recv.at[ctx_me, who],
            device_id=(source(peer), req_me), device_id_type=MESH,
        )

    def stat_arrival(peer, who):
        other = source(peer)
        return pltpu.make_async_remote_copy(
            src_ref=stats.at[other, who], dst_ref=stats.at[other, who],
            send_sem=stat_send.at[0, 0], recv_sem=stat_recv.at[other, who],
            device_id=(other, req_me), device_id_type=MESH,
        )

    def arrive(slot):
        @pl.when(slot >= units)
        def _():
            q_arrival(slot % units, source(slot // units)).wait_recv()

        if slots == key_heads:
            keys_copy(slot).wait()

    if slots != key_heads:
        for index in range(key_heads):
            keys_copy(index).wait()

    width = min(256, key_dev)
    blocks = key_dev // width
    per_block = groups // blocks

    def work(made, made_to, used, used_from):
        if made is not None:
            rows = jnp.concatenate([q_all[source(made // units), made % units], onehot[...]], axis=1)
            made_head = pl.multiple_of(key_head(made) * head_dim, LANES)
        top = jnp.zeros((SUB, LANES), jnp.float32)
        total = jnp.ones((SUB, LANES), jnp.float32)
        for index in range(blocks):
            span = pl.ds(index * width, width)
            if made is not None:
                block = jnp.concatenate(
                    [keys[span, pl.ds(made_head, head_dim)], bias[span, :]], axis=1
                )
                made_to[:, span] = lax.dot_general(
                    rows, block, (((1,), (1,)), ((), ())), preferred_element_type=jnp.float32
                )
            if used is None:
                continue
            for group in range(index * per_block, (index + 1) * per_block):
                s = used_from[pl.ds(group * SUB, SUB), :]
                highest = jnp.max(s, axis=1, keepdims=True)
                e = jnp.exp2((s - highest) * factor)
                exps[used, pl.ds(group * SUB, SUB), :] = e
                here = tile_lane == group
                top = jnp.where(here, highest, top)
                total = jnp.where(here, jnp.sum(e, axis=1, keepdims=True), total)
        if used is not None:
            who, unit = source(used // units), used % units
            stats[ctx_me, who, unit, 0] = top
            stats[ctx_me, who, unit, 1] = total

            @pl.when(unit == units - 1)
            def _():
                for peer in range(1, ctx):
                    stat_copy(used // units, peer).start()

    arrive(0)
    work(0, scores_a, None, None)

    def score_pair(pair, carry):
        used = 2 * pair
        arrive(used + 1)
        work(used + 1, scores_b, used, scores_a)
        arrive(used + 2)
        work(used + 2, scores_a, used + 1, scores_b)
        return carry

    lax.fori_loop(0, slots // 2 - 1, score_pair, 0)
    arrive(slots - 1)
    work(slots - 1, scores_b, slots - 2, scores_a)
    work(None, None, slots - 1, scores_b)

    scorer_copy.wait()
    mine = keys[pl.ds(pl.multiple_of(req_me * owned, owned), owned), :]
    projected = jnp.dot(mine, scorer_in[...], preferred_element_type=jnp.float32)
    hidden = (projected / (1.0 + jnp.exp(-projected))).astype(jnp.bfloat16)
    gating = lax.dot_general(
        scorer_out_ref[...], hidden, (((1,), (1,)), ((), ())), preferred_element_type=jnp.float32
    )
    gate[...] = 2.0 / (1.0 + jnp.exp(-gating))

    def mass_step(step, carry):
        who = source(step)
        for peer in range(1, ctx):
            stat_arrival(peer, who).wait_recv()

        def mass_unit(unit, carry):
            highest = stats[0, who, unit, 0]
            for other in range(1, ctx):
                highest = jnp.maximum(highest, stats[other, who, unit, 0])
            total = jnp.zeros((SUB, LANES), jnp.float32)
            for other in range(ctx):
                total = total + stats[other, who, unit, 1] * jnp.exp2(
                    (stats[other, who, unit, 0] - highest) * factor
                )
            weight = jnp.exp2((stats[ctx_me, who, unit, 0] - highest) * factor) / total
            slot = step * units + unit

            mass = jnp.zeros((SUB, key_dev), jnp.float32)
            for group in range(groups):
                mass = mass + exps[slot, pl.ds(group * SUB, SUB), :] * weight[:, group : group + 1]
            head = key_head(slot)
            columns[pl.ds(head, 1), :] += jnp.sum(mass, axis=0, keepdims=True)
            return carry

        return lax.fori_loop(0, units, mass_unit, carry)

    lax.fori_loop(0, ctx, mass_step, 0)

    shifted = pltpu.roll(
        jnp.concatenate([columns[...], jnp.zeros((key_heads, LANES), jnp.float32)], axis=1), RAD, 1
    )
    for r in range(req):
        pieces[r] = shifted[:, r * owned : (r + 1) * owned + LANES]

    def part_copy(step):
        to = ring(step)
        return pltpu.make_async_remote_copy(
            src_ref=pieces.at[to], dst_ref=parts.at[req_me],
            send_sem=part_send.at[step], recv_sem=part_recv.at[req_me],
            device_id=(ctx_me, to), device_id_type=MESH,
        )

    def part_arrival(step):
        other = ring(step)
        return pltpu.make_async_remote_copy(
            src_ref=pieces.at[other], dst_ref=parts.at[other],
            send_sem=part_send.at[0], recv_sem=part_recv.at[other],
            device_id=(ctx_me, other), device_id_type=MESH,
        )

    def left_copy():
        return pltpu.make_async_remote_copy(
            src_ref=pieces.at[req - 1, :, pl.ds(owned, LANES)], dst_ref=left.at[req_me],
            send_sem=left_send, recv_sem=left_recv.at[req_me],
            device_id=(ctx_me + 1, 0), device_id_type=MESH,
        )

    def right_copy():
        return pltpu.make_async_remote_copy(
            src_ref=pieces.at[0, :, pl.ds(0, LANES)], dst_ref=right.at[req_me],
            send_sem=right_send, recv_sem=right_recv.at[req_me],
            device_id=(ctx_me - 1, req - 1), device_id_type=MESH,
        )

    for step in range(1, req):
        part_copy(step).start()

    @pl.when(has_right)
    def _():
        left_copy().start()

    @pl.when(has_left)
    def _():
        right_copy().start()

    for step in range(1, req):
        part_arrival(step).wait_recv()
    summed = pieces[req_me]
    for step in range(1, req):
        summed = summed + parts[ring(step)]
    ext[...] = summed

    @pl.when(takes_left)
    def _():
        total = jnp.zeros((key_heads, LANES), jnp.float32)
        for r in range(req):
            pltpu.make_async_remote_copy(
                src_ref=left.at[r], dst_ref=left.at[r], send_sem=left_send,
                recv_sem=left_recv.at[r], device_id=(ctx_me - 1, r), device_id_type=MESH,
            ).wait_recv()
            total = total + left[r]
        ext[:, :LANES] += total

    @pl.when(takes_right)
    def _():
        total = jnp.zeros((key_heads, LANES), jnp.float32)
        for r in range(req):
            pltpu.make_async_remote_copy(
                src_ref=right.at[r], dst_ref=right.at[r], send_sem=right_send,
                recv_sem=right_recv.at[r], device_id=(ctx_me + 1, r), device_id_type=MESH,
            ).wait_recv()
            total = total + right[r]
        halo_lane = lax.broadcasted_iota(jnp.int32, (key_heads, LANES), 1)
        inside = jnp.logical_and(halo_lane >= RAD, halo_lane < 2 * RAD)
        ext[:, owned:] += jnp.where(inside, total, 0.0)

    head_row = lax.broadcasted_iota(jnp.int32, (key_heads, owned), 0)
    pool_width = jnp.ones((key_heads, owned), jnp.int32)
    for head in range(key_heads):
        pool_width = jnp.where(head_row == head, width_ref[head], pool_width)
    half = pool_width // 2
    rest = (pool_width - 1) // 2
    whole = ext[...]
    window = jnp.zeros((key_heads, owned), jnp.float32)
    for tap in range(-RAD, RAD + 1):
        moved = whole if tap == -RAD else pltpu.roll(whole, owned + LANES - RAD - tap, 1)
        inside = jnp.logical_and(tap >= -half, tap <= rest)
        window = window + jnp.where(inside, moved[:, :owned], 0.0)
    out_ref[...] = window / pool_width.astype(jnp.float32) * gate[...]

    for unit in range(units):
        for step in range(1, ctx):
            q_copy(unit, step).wait_send()

    def drain(step, carry):
        for peer in range(1, ctx):
            stat_copy(step, peer).wait_send()
        return carry

    lax.fori_loop(0, ctx, drain, 0)
    for step in range(1, req):
        part_copy(step).wait_send()

    @pl.when(has_right)
    def _():
        left_copy().wait_send()

    @pl.when(has_left)
    def _():
        right_copy().wait_send()


def per_device(
    ctx, req, queries, prefix_keys, lengths, positions, pool_width, scorer_in, scorer_out
):
    row_count, heads_here, head_dim = queries.shape
    key_heads = pool_width.shape[0]
    key_dev = prefix_keys.shape[0]
    group = heads_here * ctx // key_heads
    split = min(group, heads_here)
    units = heads_here // split
    unit_rows = row_count * split
    owned = key_dev // req
    side = math.isqrt(ctx)
    side = side if side * side == ctx else 1
    arranged = (
        queries.reshape(row_count, units, split, head_dim)
        .transpose(1, 0, 2, 3)
        .reshape(units, unit_rows, head_dim)
    )
    vmem = pl.BlockSpec(memory_space=pltpu.VMEM)
    smem = pl.BlockSpec(memory_space=pltpu.SMEM)
    anywhere = pl.BlockSpec(memory_space=pl.ANY)
    dma = pltpu.SemaphoreType.DMA
    f32, bf16 = jnp.float32, jnp.bfloat16
    return pl.pallas_call(
        functools.partial(kernel, (ctx, req, units, split, side)),
        out_shape=jax.ShapeDtypeStruct((key_heads, owned), f32),
        in_specs=[vmem, smem, vmem, smem, vmem, anywhere, anywhere],
        out_specs=vmem,
        scratch_shapes=[
            pltpu.VMEM(prefix_keys.shape, bf16),
            pltpu.VMEM(scorer_in.shape, bf16),
            pltpu.VMEM((ctx, units, unit_rows, head_dim), bf16),
            pltpu.VMEM((positions.shape[0], LANES), jnp.int32),
            pltpu.VMEM((key_dev, LANES), bf16),
            pltpu.VMEM((unit_rows, LANES), bf16),
            pltpu.VMEM((unit_rows, key_dev), f32),
            pltpu.VMEM((unit_rows, key_dev), f32),
            pltpu.VMEM((ctx * units, unit_rows, key_dev), f32),
            pltpu.VMEM((ctx, ctx, units, 2, SUB, LANES), f32),
            pltpu.VMEM((key_heads, key_dev), f32),
            pltpu.VMEM((req, key_heads, owned + LANES), f32),
            pltpu.VMEM((req, key_heads, owned + LANES), f32),
            pltpu.VMEM((req, key_heads, LANES), f32),
            pltpu.VMEM((req, key_heads, LANES), f32),
            pltpu.VMEM((key_heads, owned + LANES), f32),
            pltpu.VMEM((key_heads, owned), f32),
            dma((key_heads,)), dma, dma,
            dma((units, ctx)), dma((ctx, units)),
            dma((ctx, ctx)), dma((ctx, ctx)),
            dma((req,)), dma((req,)),
            dma, dma((req,)),
            dma, dma((req,)),
        ],
        compiler_params=pltpu.CompilerParams(
            collective_id=0, has_side_effects=True, vmem_limit_bytes=60 * 1024 * 1024
        ),
    )(arranged, lengths, positions, pool_width, scorer_out.T, prefix_keys, scorer_in)


def solution(mesh):
    placed = (P("req", "ctx", None), P("ctx", None), P("req"), P("req", None), P(), P(), P())
    body = functools.partial(per_device, mesh.shape["ctx"], mesh.shape["req"])
    return jax.shard_map(
        body, mesh=mesh, in_specs=placed, out_specs=P(None, ("ctx", "req")), check_vma=False
    )
```

```python
import functools
import math

import jax
import jax.numpy as jnp
from jax import lax
from jax.experimental import pallas as pl
from jax.experimental.pallas import tpu as pltpu
from jax.sharding import PartitionSpec as P

RAD = 3
MASKED = -1e30
LANES = 128
SUB = 8
MESH = pl.DeviceIdType.MESH


def kernel(
    sizes, q_hbm, lengths_ref, positions_ref, width_ref, scorer_out_ref, keys_hbm, scorer_in_hbm, out_ref,
    q_raw, keys, scorer_in, q_all, limits, bias, onehot, scores_a, scores_b, exps, stats, columns, pieces, parts, left, right,
    ext, gate,
    keys_sem, scorer_sem, raw_sem, q_send, q_recv, stat_send, stat_recv, part_send, part_recv,
    left_send, left_recv, right_send, right_recv,
):
    ctx, req, units, split, side = sizes
    ctx_me, req_me = lax.axis_index("ctx"), lax.axis_index("req")
    key_heads = width_ref.shape[0]
    key_dev = keys.shape[0]
    unit_rows, head_dim = q_all.shape[2:]
    groups = unit_rows // SUB
    owned = out_ref.shape[1]
    factor = math.log2(math.e) / math.sqrt(head_dim)

    def source(step):
        down, along = step // side, step % side
        row = (ctx_me // side + down) % (ctx // side)
        return row * side + (ctx_me % side + along) % side

    def ring(step):
        return (req_me + step) % req

    barrier = pltpu.get_barrier_semaphore()

    def greet(c, r):
        pl.semaphore_signal(barrier, inc=1, device_id=(c, r), device_id_type=MESH)

    for step in range(1, ctx):
        greet(source(step), req_me)
    for step in range(1, req):
        greet(ctx_me, ring(step))

    has_left = ctx_me > 0
    has_right = ctx_me < ctx - 1
    takes_left = jnp.logical_and(req_me == 0, has_left)
    takes_right = jnp.logical_and(req_me == req - 1, has_right)

    @pl.when(takes_left)
    def _():
        for r in range(1, req):
            greet(ctx_me - 1, r)

    @pl.when(takes_right)
    def _():
        for r in range(req - 1):
            greet(ctx_me + 1, r)

    if q_hbm.shape == q_all.shape[1:]:
        raw_copy = pltpu.make_async_copy(q_hbm, q_all.at[ctx_me], raw_sem)
    else:
        raw_copy = pltpu.make_async_copy(q_hbm, q_raw, raw_sem)
    raw_copy.start()
    slots = ctx * units
    heads_each = slots * split // key_heads

    def place(slot):
        later = jnp.maximum(slot - units, 0)
        own = slot < units
        unit = jnp.where(own, slot, later // (ctx - 1))
        return jnp.where(own, 0, 1 + later % (ctx - 1)), unit

    def key_head(slot):
        step, unit = place(slot)
        return ((source(step) * units + unit) * split) // heads_each

    def keys_copy(index):
        head = key_head(index) if slots == key_heads else index
        span = pl.ds(pl.multiple_of(head * head_dim, LANES), head_dim)
        return pltpu.make_async_copy(keys_hbm.at[:, span], keys.at[:, span], keys_sem.at[index])

    for index in range(key_heads):
        keys_copy(index).start()
    scorer_copy = pltpu.make_async_copy(scorer_in_hbm, scorer_in, scorer_sem)
    scorer_copy.start()
    lane_keys = ctx_me * key_dev + lax.broadcasted_iota(jnp.int32, (key_dev, LANES), 0)
    requests, window_rows = positions_ref.shape
    limits[...] = jnp.zeros_like(limits)
    for i in range(requests):
        limits[i : i + 1, :window_rows] = jnp.minimum(
            positions_ref[i : i + 1, :], lengths_ref[i] - 1
        )
    limit = limits[0:1, :]
    for i in range(1, requests):
        limit = limit + pltpu.roll(limits[i : i + 1, :], i * window_rows, 1)
    bias[...] = jnp.where(lane_keys <= limit, 0.0, MASKED).astype(jnp.bfloat16)
    row = lax.broadcasted_iota(jnp.int32, (unit_rows, LANES), 0)
    lane = lax.broadcasted_iota(jnp.int32, (unit_rows, LANES), 1)
    first = lane * split
    onehot[...] = jnp.where(
        jnp.logical_and(row >= first, row < first + split), 1.0, 0.0
    ).astype(jnp.bfloat16)
    columns[...] = jnp.zeros_like(columns)

    raw_copy.wait()
    if q_hbm.shape != q_all.shape[1:]:
        wide = q_raw[...].astype(jnp.float32)
        for unit in range(units):
            part = wide[:, unit * split : (unit + 1) * split, :]
            q_all[ctx_me, unit] = part.reshape(unit_rows, head_dim).astype(jnp.bfloat16)

    extra_right = jnp.logical_and(has_right, req_me != 0)
    extra_left = jnp.logical_and(has_left, req_me != req - 1)
    extra = extra_right.astype(jnp.int32) + extra_left.astype(jnp.int32)
    pl.semaphore_wait(barrier, ctx - 1 + req - 1 + extra)

    def q_copy(unit, step):
        return pltpu.make_async_remote_copy(
            src_ref=q_all.at[ctx_me, unit], dst_ref=q_all.at[ctx_me, unit],
            send_sem=q_send.at[unit, step], recv_sem=q_recv.at[ctx_me, unit],
            device_id=(source(step), req_me), device_id_type=MESH,
        )

    def q_arrival(unit, who):
        return pltpu.make_async_remote_copy(
            src_ref=q_all.at[ctx_me, unit], dst_ref=q_all.at[who, unit],
            send_sem=q_send.at[unit, 0], recv_sem=q_recv.at[who, unit],
            device_id=(who, req_me), device_id_type=MESH,
        )

    for unit in range(units):
        for step in range(1, ctx):
            q_copy(unit, step).start()


    tile_lane = lax.broadcasted_iota(jnp.int32, (SUB, LANES), 1)

    def stat_copy(slot, peer):
        step, unit = place(slot)
        who = source(step)
        return pltpu.make_async_remote_copy(
            src_ref=stats.at[ctx_me, who, unit], dst_ref=stats.at[ctx_me, who, unit],
            send_sem=stat_send.at[slot, peer], recv_sem=stat_recv.at[ctx_me, who, unit],
            device_id=(source(peer), req_me), device_id_type=MESH,
        )

    def stat_arrival(peer, who, unit):
        other = source(peer)
        return pltpu.make_async_remote_copy(
            src_ref=stats.at[other, who, unit], dst_ref=stats.at[other, who, unit],
            send_sem=stat_send.at[0, 0], recv_sem=stat_recv.at[other, who, unit],
            device_id=(other, req_me), device_id_type=MESH,
        )

    def arrive(slot):
        @pl.when(slot >= units)
        def _():
            step, unit = place(slot)
            q_arrival(unit, source(step)).wait_recv()

        if slots == key_heads:
            keys_copy(slot).wait()

    if slots != key_heads:
        for index in range(key_heads):
            keys_copy(index).wait()

    width = min(256, key_dev)
    blocks = key_dev // width
    per_block = groups // blocks

    def work(made, made_to, used, used_from):
        if made is not None:
            made_step, made_unit = place(made)
            rows = jnp.concatenate([q_all[source(made_step), made_unit], onehot[...]], axis=1)
            made_head = pl.multiple_of(key_head(made) * head_dim, LANES)
        top = jnp.zeros((SUB, LANES), jnp.float32)
        total = jnp.ones((SUB, LANES), jnp.float32)
        for index in range(blocks):
            span = pl.ds(index * width, width)
            if made is not None:
                block = jnp.concatenate(
                    [keys[span, pl.ds(made_head, head_dim)], bias[span, :]], axis=1
                )
                made_to[:, span] = lax.dot_general(
                    rows, block, (((1,), (1,)), ((), ())), preferred_element_type=jnp.float32
                )
            if used is None:
                continue
            for group in range(index * per_block, (index + 1) * per_block):
                s = used_from[pl.ds(group * SUB, SUB), :]
                highest = jnp.max(s, axis=1, keepdims=True)
                e = jnp.exp2((s - highest) * factor)
                exps[used, pl.ds(group * SUB, SUB), :] = e
                here = tile_lane == group
                top = jnp.where(here, highest, top)
                total = jnp.where(here, jnp.sum(e, axis=1, keepdims=True), total)
        if used is not None:
            step, unit = place(used)
            who = source(step)
            stats[ctx_me, who, unit, 0] = top
            stats[ctx_me, who, unit, 1] = total
            for peer in range(1, ctx):
                stat_copy(used, peer).start()

    arrive(0)
    work(0, scores_a, None, None)

    def score_pair(pair, carry):
        used = 2 * pair
        arrive(used + 1)
        work(used + 1, scores_b, used, scores_a)
        arrive(used + 2)
        work(used + 2, scores_a, used + 1, scores_b)
        return carry

    lax.fori_loop(0, slots // 2 - 1, score_pair, 0)
    arrive(slots - 1)
    work(slots - 1, scores_b, slots - 2, scores_a)
    work(None, None, slots - 1, scores_b)

    def mass_step(index, carry):
        unit, step = index // ctx, index % ctx
        who = source(step)
        for peer in range(1, ctx):
            stat_arrival(peer, who, unit).wait_recv()
        highest = stats[0, who, unit, 0]
        for other in range(1, ctx):
            highest = jnp.maximum(highest, stats[other, who, unit, 0])
        total = jnp.zeros((SUB, LANES), jnp.float32)
        for other in range(ctx):
            total = total + stats[other, who, unit, 1] * jnp.exp2(
                (stats[other, who, unit, 0] - highest) * factor
            )
        weight = jnp.exp2((stats[ctx_me, who, unit, 0] - highest) * factor) / total
        slot = jnp.where(step == 0, unit, units + unit * (ctx - 1) + step - 1)

        mass = jnp.zeros((SUB, key_dev), jnp.float32)
        for group in range(groups):
            mass = mass + exps[slot, pl.ds(group * SUB, SUB), :] * weight[:, group : group + 1]
        head = key_head(slot)
        columns[pl.ds(head, 1), :] += jnp.sum(mass, axis=0, keepdims=True)
        return carry

    lax.fori_loop(0, slots, mass_step, 0)

    shifted = pltpu.roll(
        jnp.concatenate([columns[...], jnp.zeros((key_heads, LANES), jnp.float32)], axis=1), RAD, 1
    )
    for r in range(req):
        pieces[r] = shifted[:, r * owned : (r + 1) * owned + LANES]

    def part_copy(step):
        to = ring(step)
        return pltpu.make_async_remote_copy(
            src_ref=pieces.at[to], dst_ref=parts.at[req_me],
            send_sem=part_send.at[step], recv_sem=part_recv.at[req_me],
            device_id=(ctx_me, to), device_id_type=MESH,
        )

    def part_arrival(step):
        other = ring(step)
        return pltpu.make_async_remote_copy(
            src_ref=pieces.at[other], dst_ref=parts.at[other],
            send_sem=part_send.at[0], recv_sem=part_recv.at[other],
            device_id=(ctx_me, other), device_id_type=MESH,
        )

    def left_copy():
        return pltpu.make_async_remote_copy(
            src_ref=pieces.at[req - 1, :, pl.ds(owned, LANES)], dst_ref=left.at[req_me],
            send_sem=left_send, recv_sem=left_recv.at[req_me],
            device_id=(ctx_me + 1, 0), device_id_type=MESH,
        )

    def right_copy():
        return pltpu.make_async_remote_copy(
            src_ref=pieces.at[0, :, pl.ds(0, LANES)], dst_ref=right.at[req_me],
            send_sem=right_send, recv_sem=right_recv.at[req_me],
            device_id=(ctx_me - 1, req - 1), device_id_type=MESH,
        )

    for step in range(1, req):
        part_copy(step).start()

    @pl.when(has_right)
    def _():
        left_copy().start()

    @pl.when(has_left)
    def _():
        right_copy().start()

    scorer_copy.wait()
    mine = keys[pl.ds(pl.multiple_of(req_me * owned, owned), owned), :]
    projected = jnp.dot(mine, scorer_in[...], preferred_element_type=jnp.float32)
    hidden = (projected / (1.0 + jnp.exp(-projected))).astype(jnp.bfloat16)
    gating = lax.dot_general(
        scorer_out_ref[...], hidden, (((1,), (1,)), ((), ())), preferred_element_type=jnp.float32
    )
    gate[...] = 2.0 / (1.0 + jnp.exp(-gating))

    for step in range(1, req):
        part_arrival(step).wait_recv()
    summed = pieces[req_me]
    for step in range(1, req):
        summed = summed + parts[ring(step)]
    ext[...] = summed

    @pl.when(takes_left)
    def _():
        total = jnp.zeros((key_heads, LANES), jnp.float32)
        for r in range(req):
            pltpu.make_async_remote_copy(
                src_ref=left.at[r], dst_ref=left.at[r], send_sem=left_send,
                recv_sem=left_recv.at[r], device_id=(ctx_me - 1, r), device_id_type=MESH,
            ).wait_recv()
            total = total + left[r]
        ext[:, :LANES] += total

    @pl.when(takes_right)
    def _():
        total = jnp.zeros((key_heads, LANES), jnp.float32)
        for r in range(req):
            pltpu.make_async_remote_copy(
                src_ref=right.at[r], dst_ref=right.at[r], send_sem=right_send,
                recv_sem=right_recv.at[r], device_id=(ctx_me + 1, r), device_id_type=MESH,
            ).wait_recv()
            total = total + right[r]
        halo_lane = lax.broadcasted_iota(jnp.int32, (key_heads, LANES), 1)
        inside = jnp.logical_and(halo_lane >= RAD, halo_lane < 2 * RAD)
        ext[:, owned:] += jnp.where(inside, total, 0.0)

    head_row = lax.broadcasted_iota(jnp.int32, (key_heads, owned), 0)
    pool_width = jnp.ones((key_heads, owned), jnp.int32)
    for head in range(key_heads):
        pool_width = jnp.where(head_row == head, width_ref[head], pool_width)
    half = pool_width // 2
    rest = (pool_width - 1) // 2
    whole = ext[...]
    window = jnp.zeros((key_heads, owned), jnp.float32)
    for tap in range(-RAD, RAD + 1):
        moved = whole if tap == -RAD else pltpu.roll(whole, owned + LANES - RAD - tap, 1)
        inside = jnp.logical_and(tap >= -half, tap <= rest)
        window = window + jnp.where(inside, moved[:, :owned], 0.0)
    out_ref[...] = window / pool_width.astype(jnp.float32) * gate[...]

    for unit in range(units):
        for step in range(1, ctx):
            q_copy(unit, step).wait_send()

    def drain(slot, carry):
        for peer in range(1, ctx):
            stat_copy(slot, peer).wait_send()
        return carry

    lax.fori_loop(0, slots, drain, 0)
    for step in range(1, req):
        part_copy(step).wait_send()

    @pl.when(has_right)
    def _():
        left_copy().wait_send()

    @pl.when(has_left)
    def _():
        right_copy().wait_send()


def per_device(
    ctx, req, queries, prefix_keys, lengths, positions, pool_width, scorer_in, scorer_out
):
    row_count, heads_here, head_dim = queries.shape
    key_heads = pool_width.shape[0]
    key_dev = prefix_keys.shape[0]
    group = heads_here * ctx // key_heads
    split = min(group, heads_here)
    units = heads_here // split
    unit_rows = row_count * split
    owned = key_dev // req
    side = math.isqrt(ctx)
    side = side if side * side == ctx else 1
    arranged = queries
    if split != SUB:
        arranged = (
            queries.reshape(row_count, units, split, head_dim)
            .transpose(1, 0, 2, 3)
            .reshape(units, unit_rows, head_dim)
        )
    vmem = pl.BlockSpec(memory_space=pltpu.VMEM)
    smem = pl.BlockSpec(memory_space=pltpu.SMEM)
    anywhere = pl.BlockSpec(memory_space=pl.ANY)
    dma = pltpu.SemaphoreType.DMA
    f32, bf16 = jnp.float32, jnp.bfloat16
    return pl.pallas_call(
        functools.partial(kernel, (ctx, req, units, split, side)),
        out_shape=jax.ShapeDtypeStruct((key_heads, owned), f32),
        in_specs=[anywhere, smem, vmem, smem, vmem, anywhere, anywhere],
        out_specs=vmem,
        scratch_shapes=[
            pltpu.VMEM(queries.shape, bf16),
            pltpu.VMEM(prefix_keys.shape, bf16),
            pltpu.VMEM(scorer_in.shape, bf16),
            pltpu.VMEM((ctx, units, unit_rows, head_dim), bf16),
            pltpu.VMEM((positions.shape[0], LANES), jnp.int32),
            pltpu.VMEM((key_dev, LANES), bf16),
            pltpu.VMEM((unit_rows, LANES), bf16),
            pltpu.VMEM((unit_rows, key_dev), f32),
            pltpu.VMEM((unit_rows, key_dev), f32),
            pltpu.VMEM((ctx * units, unit_rows, key_dev), f32),
            pltpu.VMEM((ctx, ctx, units, 2, SUB, LANES), f32),
            pltpu.VMEM((key_heads, key_dev), f32),
            pltpu.VMEM((req, key_heads, owned + LANES), f32),
            pltpu.VMEM((req, key_heads, owned + LANES), f32),
            pltpu.VMEM((req, key_heads, LANES), f32),
            pltpu.VMEM((req, key_heads, LANES), f32),
            pltpu.VMEM((key_heads, owned + LANES), f32),
            pltpu.VMEM((key_heads, owned), f32),
            dma((key_heads,)), dma, dma,
            dma((units, ctx)), dma((ctx, units)),
            dma((ctx * units, ctx)), dma((ctx, ctx, units)),
            dma((req,)), dma((req,)),
            dma, dma((req,)),
            dma, dma((req,)),
        ],
        compiler_params=pltpu.CompilerParams(
            collective_id=0, has_side_effects=True, vmem_limit_bytes=60 * 1024 * 1024
        ),
    )(arranged, lengths, positions, pool_width, scorer_out.T, prefix_keys, scorer_in)


def solution(mesh):
    placed = (P("req", "ctx", None), P("ctx", None), P("req"), P("req", None), P(), P(), P())
    body = functools.partial(per_device, mesh.shape["ctx"], mesh.shape["req"])
    return jax.shard_map(
        body, mesh=mesh, in_specs=placed, out_specs=P(None, ("ctx", "req")), check_vma=False
    )
```

```python
import functools
import math

import jax
import jax.numpy as jnp
from jax import lax
from jax.experimental import pallas as pl
from jax.experimental.pallas import tpu as pltpu
from jax.sharding import PartitionSpec as P

RAD = 3
MASKED = -1e30
LANES = 128
SUB = 8
MESH = pl.DeviceIdType.MESH


def kernel(
    sizes, q_hbm, lengths_ref, positions_ref, width_ref, scorer_out_ref, keys_hbm, scorer_in_hbm, out_ref,
    q_raw, keys, scorer_in, q_all, limits, bias, onehot, scores_a, scores_b, exps, stats, columns, pieces, parts, left, right,
    ext, gate,
    keys_sem, scorer_sem, raw_sem, q_send, q_recv, stat_send, stat_recv, part_send, part_recv,
    left_send, left_recv, right_send, right_recv,
):
    ctx, req, units, split, side = sizes
    ctx_me, req_me = lax.axis_index("ctx"), lax.axis_index("req")
    key_heads = width_ref.shape[0]
    key_dev = keys.shape[0]
    unit_rows, head_dim = q_all.shape[2:]
    groups = unit_rows // SUB
    owned = out_ref.shape[1]
    factor = math.log2(math.e) / math.sqrt(head_dim)

    def source(step):
        down, along = step // side, step % side
        row = (ctx_me // side + down) % (ctx // side)
        return row * side + (ctx_me % side + along) % side

    def ring(step):
        return (req_me + step) % req

    barrier = pltpu.get_barrier_semaphore()

    def greet(c, r):
        pl.semaphore_signal(barrier, inc=1, device_id=(c, r), device_id_type=MESH)

    for step in range(1, ctx):
        greet(source(step), req_me)
    for step in range(1, req):
        greet(ctx_me, ring(step))

    has_left = ctx_me > 0
    has_right = ctx_me < ctx - 1
    takes_left = jnp.logical_and(req_me == 0, has_left)
    takes_right = jnp.logical_and(req_me == req - 1, has_right)

    @pl.when(takes_left)
    def _():
        for r in range(1, req):
            greet(ctx_me - 1, r)

    @pl.when(takes_right)
    def _():
        for r in range(req - 1):
            greet(ctx_me + 1, r)

    if q_hbm.shape == q_all.shape[1:]:
        raw_copy = pltpu.make_async_copy(q_hbm, q_all.at[ctx_me], raw_sem)
    else:
        raw_copy = pltpu.make_async_copy(q_hbm, q_raw, raw_sem)
    raw_copy.start()
    slots = ctx * units
    heads_each = slots * split // key_heads

    def place(slot):
        later = jnp.maximum(slot - units, 0)
        own = slot < units
        unit = jnp.where(own, slot, later // (ctx - 1))
        return jnp.where(own, 0, 1 + later % (ctx - 1)), unit

    def key_head(slot):
        step, unit = place(slot)
        return ((source(step) * units + unit) * split) // heads_each

    def keys_copy(index):
        head = key_head(index) if slots == key_heads else index
        span = pl.ds(pl.multiple_of(head * head_dim, LANES), head_dim)
        return pltpu.make_async_copy(keys_hbm.at[:, span], keys.at[:, span], keys_sem.at[index])

    for index in range(key_heads):
        keys_copy(index).start()
    scorer_copy = pltpu.make_async_copy(scorer_in_hbm, scorer_in, scorer_sem)
    scorer_copy.start()
    raw_copy.wait()
    if q_hbm.shape != q_all.shape[1:]:
        wide = q_raw[...].astype(jnp.float32)
        for unit in range(units):
            part = wide[:, unit * split : (unit + 1) * split, :]
            q_all[ctx_me, unit] = part.reshape(unit_rows, head_dim).astype(jnp.bfloat16)

    extra_right = jnp.logical_and(has_right, req_me != 0)
    extra_left = jnp.logical_and(has_left, req_me != req - 1)
    extra = extra_right.astype(jnp.int32) + extra_left.astype(jnp.int32)
    pl.semaphore_wait(barrier, ctx - 1 + req - 1 + extra)

    def q_copy(unit, step):
        return pltpu.make_async_remote_copy(
            src_ref=q_all.at[ctx_me, unit], dst_ref=q_all.at[ctx_me, unit],
            send_sem=q_send.at[unit, step], recv_sem=q_recv.at[ctx_me, unit],
            device_id=(source(step), req_me), device_id_type=MESH,
        )

    def q_arrival(unit, who):
        return pltpu.make_async_remote_copy(
            src_ref=q_all.at[ctx_me, unit], dst_ref=q_all.at[who, unit],
            send_sem=q_send.at[unit, 0], recv_sem=q_recv.at[who, unit],
            device_id=(who, req_me), device_id_type=MESH,
        )

    for unit in range(units):
        for step in range(1, ctx):
            q_copy(unit, step).start()

    lane_keys = ctx_me * key_dev + lax.broadcasted_iota(jnp.int32, (key_dev, LANES), 0)
    requests, window_rows = positions_ref.shape
    limits[...] = jnp.zeros_like(limits)
    for i in range(requests):
        limits[i : i + 1, :window_rows] = jnp.minimum(
            positions_ref[i : i + 1, :], lengths_ref[i] - 1
        )
    limit = limits[0:1, :]
    for i in range(1, requests):
        limit = limit + pltpu.roll(limits[i : i + 1, :], i * window_rows, 1)
    bias[...] = jnp.where(lane_keys <= limit, 0.0, MASKED).astype(jnp.bfloat16)
    row = lax.broadcasted_iota(jnp.int32, (unit_rows, LANES), 0)
    lane = lax.broadcasted_iota(jnp.int32, (unit_rows, LANES), 1)
    first = lane * split
    onehot[...] = jnp.where(
        jnp.logical_and(row >= first, row < first + split), 1.0, 0.0
    ).astype(jnp.bfloat16)
    columns[...] = jnp.zeros_like(columns)

    tile_lane = lax.broadcasted_iota(jnp.int32, (SUB, LANES), 1)

    def stat_copy(slot, peer):
        step, unit = place(slot)
        who = source(step)
        return pltpu.make_async_remote_copy(
            src_ref=stats.at[ctx_me, who, unit], dst_ref=stats.at[ctx_me, who, unit],
            send_sem=stat_send.at[slot, peer], recv_sem=stat_recv.at[ctx_me, who, unit],
            device_id=(source(peer), req_me), device_id_type=MESH,
        )

    def stat_arrival(peer, who, unit):
        other = source(peer)
        return pltpu.make_async_remote_copy(
            src_ref=stats.at[other, who, unit], dst_ref=stats.at[other, who, unit],
            send_sem=stat_send.at[0, 0], recv_sem=stat_recv.at[other, who, unit],
            device_id=(other, req_me), device_id_type=MESH,
        )

    def arrive(slot):
        @pl.when(slot >= units)
        def _():
            step, unit = place(slot)
            q_arrival(unit, source(step)).wait_recv()

        if slots == key_heads:
            keys_copy(slot).wait()

    if slots != key_heads:
        for index in range(key_heads):
            keys_copy(index).wait()

    width = min(256, key_dev)
    blocks = key_dev // width
    per_block = groups // blocks

    def work(made, made_to, used, used_from):
        if made is not None:
            made_step, made_unit = place(made)
            rows = jnp.concatenate([q_all[source(made_step), made_unit], onehot[...]], axis=1)
            made_head = pl.multiple_of(key_head(made) * head_dim, LANES)
        top = jnp.zeros((SUB, LANES), jnp.float32)
        total = jnp.ones((SUB, LANES), jnp.float32)
        for index in range(blocks):
            span = pl.ds(index * width, width)
            if made is not None:
                block = jnp.concatenate(
                    [keys[span, pl.ds(made_head, head_dim)], bias[span, :]], axis=1
                )
                made_to[:, span] = lax.dot_general(
                    rows, block, (((1,), (1,)), ((), ())), preferred_element_type=jnp.float32
                )
            if used is None:
                continue
            for group in range(index * per_block, (index + 1) * per_block):
                s = used_from[pl.ds(group * SUB, SUB), :]
                highest = jnp.max(s, axis=1, keepdims=True)
                e = jnp.exp2((s - highest) * factor)
                exps[used, pl.ds(group * SUB, SUB), :] = e
                here = tile_lane == group
                top = jnp.where(here, highest, top)
                total = jnp.where(here, jnp.sum(e, axis=1, keepdims=True), total)
        if used is not None:
            step, unit = place(used)
            who = source(step)
            stats[ctx_me, who, unit, 0] = top
            stats[ctx_me, who, unit, 1] = total
            for peer in range(1, ctx):
                stat_copy(used, peer).start()

    arrive(0)
    work(0, scores_a, None, None)

    def score_pair(pair, carry):
        used = 2 * pair
        arrive(used + 1)
        work(used + 1, scores_b, used, scores_a)
        arrive(used + 2)
        work(used + 2, scores_a, used + 1, scores_b)
        return carry

    lax.fori_loop(0, slots // 2 - 1, score_pair, 0)
    arrive(slots - 1)
    work(slots - 1, scores_b, slots - 2, scores_a)
    work(None, None, slots - 1, scores_b)

    def mass_step(index, carry):
        unit, step = index // ctx, index % ctx
        who = source(step)
        for peer in range(1, ctx):
            stat_arrival(peer, who, unit).wait_recv()
        highest = stats[0, who, unit, 0]
        for other in range(1, ctx):
            highest = jnp.maximum(highest, stats[other, who, unit, 0])
        total = jnp.zeros((SUB, LANES), jnp.float32)
        for other in range(ctx):
            total = total + stats[other, who, unit, 1] * jnp.exp2(
                (stats[other, who, unit, 0] - highest) * factor
            )
        weight = jnp.exp2((stats[ctx_me, who, unit, 0] - highest) * factor) / total
        slot = jnp.where(step == 0, unit, units + unit * (ctx - 1) + step - 1)

        mass = jnp.zeros((SUB, key_dev), jnp.float32)
        for group in range(groups):
            mass = mass + exps[slot, pl.ds(group * SUB, SUB), :] * weight[:, group : group + 1]
        head = key_head(slot)
        columns[pl.ds(head, 1), :] += jnp.sum(mass, axis=0, keepdims=True)
        return carry

    lax.fori_loop(0, slots, mass_step, 0)

    shifted = pltpu.roll(
        jnp.concatenate([columns[...], jnp.zeros((key_heads, LANES), jnp.float32)], axis=1), RAD, 1
    )
    for r in range(req):
        pieces[r] = shifted[:, r * owned : (r + 1) * owned + LANES]

    def part_copy(step):
        to = ring(step)
        return pltpu.make_async_remote_copy(
            src_ref=pieces.at[to], dst_ref=parts.at[req_me],
            send_sem=part_send.at[step], recv_sem=part_recv.at[req_me],
            device_id=(ctx_me, to), device_id_type=MESH,
        )

    def part_arrival(step):
        other = ring(step)
        return pltpu.make_async_remote_copy(
            src_ref=pieces.at[other], dst_ref=parts.at[other],
            send_sem=part_send.at[0], recv_sem=part_recv.at[other],
            device_id=(ctx_me, other), device_id_type=MESH,
        )

    def left_copy():
        return pltpu.make_async_remote_copy(
            src_ref=pieces.at[req - 1, :, pl.ds(owned, LANES)], dst_ref=left.at[req_me],
            send_sem=left_send, recv_sem=left_recv.at[req_me],
            device_id=(ctx_me + 1, 0), device_id_type=MESH,
        )

    def right_copy():
        return pltpu.make_async_remote_copy(
            src_ref=pieces.at[0, :, pl.ds(0, LANES)], dst_ref=right.at[req_me],
            send_sem=right_send, recv_sem=right_recv.at[req_me],
            device_id=(ctx_me - 1, req - 1), device_id_type=MESH,
        )

    for step in range(1, req):
        part_copy(step).start()

    @pl.when(has_right)
    def _():
        left_copy().start()

    @pl.when(has_left)
    def _():
        right_copy().start()

    scorer_copy.wait()
    mine = keys[pl.ds(pl.multiple_of(req_me * owned, owned), owned), :]
    projected = jnp.dot(mine, scorer_in[...], preferred_element_type=jnp.float32)
    hidden = (projected / (1.0 + jnp.exp(-projected))).astype(jnp.bfloat16)
    gating = lax.dot_general(
        scorer_out_ref[...], hidden, (((1,), (1,)), ((), ())), preferred_element_type=jnp.float32
    )
    gate[...] = 2.0 / (1.0 + jnp.exp(-gating))

    for step in range(1, req):
        part_arrival(step).wait_recv()
    summed = pieces[req_me]
    for step in range(1, req):
        summed = summed + parts[ring(step)]
    ext[...] = summed

    @pl.when(takes_left)
    def _():
        total = jnp.zeros((key_heads, LANES), jnp.float32)
        for r in range(req):
            pltpu.make_async_remote_copy(
                src_ref=left.at[r], dst_ref=left.at[r], send_sem=left_send,
                recv_sem=left_recv.at[r], device_id=(ctx_me - 1, r), device_id_type=MESH,
            ).wait_recv()
            total = total + left[r]
        ext[:, :LANES] += total

    @pl.when(takes_right)
    def _():
        total = jnp.zeros((key_heads, LANES), jnp.float32)
        for r in range(req):
            pltpu.make_async_remote_copy(
                src_ref=right.at[r], dst_ref=right.at[r], send_sem=right_send,
                recv_sem=right_recv.at[r], device_id=(ctx_me + 1, r), device_id_type=MESH,
            ).wait_recv()
            total = total + right[r]
        halo_lane = lax.broadcasted_iota(jnp.int32, (key_heads, LANES), 1)
        inside = jnp.logical_and(halo_lane >= RAD, halo_lane < 2 * RAD)
        ext[:, owned:] += jnp.where(inside, total, 0.0)

    head_row = lax.broadcasted_iota(jnp.int32, (key_heads, owned), 0)
    pool_width = jnp.ones((key_heads, owned), jnp.int32)
    for head in range(key_heads):
        pool_width = jnp.where(head_row == head, width_ref[head], pool_width)
    half = pool_width // 2
    rest = (pool_width - 1) // 2
    whole = ext[...]
    window = jnp.zeros((key_heads, owned), jnp.float32)
    for tap in range(-RAD, RAD + 1):
        moved = whole if tap == -RAD else pltpu.roll(whole, owned + LANES - RAD - tap, 1)
        inside = jnp.logical_and(tap >= -half, tap <= rest)
        window = window + jnp.where(inside, moved[:, :owned], 0.0)
    out_ref[...] = window / pool_width.astype(jnp.float32) * gate[...]

    for unit in range(units):
        for step in range(1, ctx):
            q_copy(unit, step).wait_send()

    def drain(slot, carry):
        for peer in range(1, ctx):
            stat_copy(slot, peer).wait_send()
        return carry

    lax.fori_loop(0, slots, drain, 0)
    for step in range(1, req):
        part_copy(step).wait_send()

    @pl.when(has_right)
    def _():
        left_copy().wait_send()

    @pl.when(has_left)
    def _():
        right_copy().wait_send()


def per_device(
    ctx, req, queries, prefix_keys, lengths, positions, pool_width, scorer_in, scorer_out
):
    row_count, heads_here, head_dim = queries.shape
    key_heads = pool_width.shape[0]
    key_dev = prefix_keys.shape[0]
    group = heads_here * ctx // key_heads
    split = min(group, heads_here)
    units = heads_here // split
    unit_rows = row_count * split
    owned = key_dev // req
    side = math.isqrt(ctx)
    side = side if side * side == ctx else 1
    arranged = queries
    if split != SUB:
        arranged = (
            queries.reshape(row_count, units, split, head_dim)
            .transpose(1, 0, 2, 3)
            .reshape(units, unit_rows, head_dim)
        )
    vmem = pl.BlockSpec(memory_space=pltpu.VMEM)
    smem = pl.BlockSpec(memory_space=pltpu.SMEM)
    anywhere = pl.BlockSpec(memory_space=pl.ANY)
    dma = pltpu.SemaphoreType.DMA
    f32, bf16 = jnp.float32, jnp.bfloat16
    return pl.pallas_call(
        functools.partial(kernel, (ctx, req, units, split, side)),
        out_shape=jax.ShapeDtypeStruct((key_heads, owned), f32),
        in_specs=[anywhere, smem, vmem, smem, vmem, anywhere, anywhere],
        out_specs=vmem,
        scratch_shapes=[
            pltpu.VMEM(queries.shape, bf16),
            pltpu.VMEM(prefix_keys.shape, bf16),
            pltpu.VMEM(scorer_in.shape, bf16),
            pltpu.VMEM((ctx, units, unit_rows, head_dim), bf16),
            pltpu.VMEM((positions.shape[0], LANES), jnp.int32),
            pltpu.VMEM((key_dev, LANES), bf16),
            pltpu.VMEM((unit_rows, LANES), bf16),
            pltpu.VMEM((unit_rows, key_dev), f32),
            pltpu.VMEM((unit_rows, key_dev), f32),
            pltpu.VMEM((ctx * units, unit_rows, key_dev), f32),
            pltpu.VMEM((ctx, ctx, units, 2, SUB, LANES), f32),
            pltpu.VMEM((key_heads, key_dev), f32),
            pltpu.VMEM((req, key_heads, owned + LANES), f32),
            pltpu.VMEM((req, key_heads, owned + LANES), f32),
            pltpu.VMEM((req, key_heads, LANES), f32),
            pltpu.VMEM((req, key_heads, LANES), f32),
            pltpu.VMEM((key_heads, owned + LANES), f32),
            pltpu.VMEM((key_heads, owned), f32),
            dma((key_heads,)), dma, dma,
            dma((units, ctx)), dma((ctx, units)),
            dma((ctx * units, ctx)), dma((ctx, ctx, units)),
            dma((req,)), dma((req,)),
            dma, dma((req,)),
            dma, dma((req,)),
        ],
        compiler_params=pltpu.CompilerParams(
            collective_id=0, has_side_effects=True, vmem_limit_bytes=60 * 1024 * 1024
        ),
    )(arranged, lengths, positions, pool_width, scorer_out.T, prefix_keys, scorer_in)


def solution(mesh):
    placed = (P("req", "ctx", None), P("ctx", None), P("req"), P("req", None), P(), P(), P())
    body = functools.partial(per_device, mesh.shape["ctx"], mesh.shape["req"])
    return jax.shard_map(
        body, mesh=mesh, in_specs=placed, out_specs=P(None, ("ctx", "req")), check_vma=False
    )
```
